32 devices in a mesh: ctx: 4 (over y, core), uly: 8 (over z, x).
Axes of the slice: x: 2, y: 2, z: 4, core: 2. Of those that a mesh axis runs over, the one named last changes fastest.
Arguments:
- query: bfloat16 [4096, 5120], P(('ctx', 'uly')), may hold values from -8 to 8
- key: bfloat16 [4096, 5120], P(('ctx', 'uly')), may hold values from -8 to 8
- value: bfloat16 [4096, 5120], P(('ctx', 'uly')), may hold values from -6 to 6
- dout: bfloat16 [4096, 5120], P(('ctx', 'uly')), may hold values from -6 to 6
- tile_mask: int32 [40, 32, 5], replicated, may hold values from 0 to 1, as said below
Outputs:
- grad_query: bfloat16 [4096, 5120], P(('ctx', 'uly'))
- grad_key: bfloat16 [4096, 5120], P(('ctx', 'uly'))
- grad_value: bfloat16 [4096, 5120], P(('ctx', 'uly'))
The draws below stay inside these ranges and needn't reach their ends.
Inputs may be any that keep to these rules, and one draw needn't show every extreme that they name: `tile_mask`: the tile of a block with itself (offset 2) is active for every head and block.
All inputs are finite; a program needn't handle non-finite values.
Results may differ from the reference program's by a relative error of at most 0.0053.
Values may be sent and summed in bfloat16 or wider, within the bound.
A program may use at most 128 MiB of HBM per device.

```python
import math
import jax
import jax.numpy as jnp
from jax import lax

H = 40
HD = 128
D = 5120
BLK = 128
W = 2
TOKENS = 4096


def draw_query(key, part):
    noise = jax.random.normal(jax.random.fold_in(key, 1), (TOKENS, H * HD), jnp.float32)
    return jnp.clip(noise, -6.0, 6.0).astype(jnp.bfloat16)


def draw_key(key, part):
    noise = jax.random.normal(jax.random.fold_in(key, 2), (TOKENS, H * HD), jnp.float32)
    return jnp.clip(noise, -6.0, 6.0).astype(jnp.bfloat16)


def draw_tile_mask(key, part):
    density = jax.random.randint(jax.random.fold_in(key, 1), (H, 1, 1), 3, 11)
    tile_rolls = jax.random.randint(jax.random.fold_in(key, 2), (H, TOKENS // BLK, 2 * W + 1), 0, 10)
    tile_draw = (tile_rolls < density).astype(jnp.int32)
    on_diagonal = jnp.arange(2 * W + 1) == W
    return jnp.where(on_diagonal[None, None, :], 1, tile_draw).astype(jnp.int32)


def block_scale(own_key, shape, split, low, high):
    loudness = 1.0
    for position, parts in split:
        heights = jax.random.uniform(jax.random.fold_in(jax.random.fold_in(own_key, 6), position), (parts,), jnp.float32, low / len(split), high / len(split))
        loudness = loudness * jnp.repeat(jnp.exp(heights), shape[position] // parts).reshape((-1,) + (1,) * (len(shape) - 1 - position))
    return loudness


def scatter_about(stream_key, shape, width, reach, pieces=(), held_as=jnp.bfloat16):
    values = width * jax.random.normal(stream_key, shape, jnp.float32)
    if pieces:
        values = values * block_scale(stream_key, shape, pieces, -0.22, 0.18)
    return jnp.clip(values, -reach, reach).astype(held_as)


def setup_inputs(seed: int = 0) -> dict:
    arg_keys = jax.random.split(jax.random.key(seed), 6)
    return {
        "query": draw_query(jax.random.fold_in(arg_keys[5], 71), 0),
        "key": draw_key(jax.random.fold_in(arg_keys[5], 71), 0),
        "value": scatter_about(arg_keys[2], (TOKENS, D), 1.0, 6.0, ((0, 32),)),
        "dout": scatter_about(arg_keys[3], (TOKENS, D), 1.0, 6.0, ((0, 32),)),
        "tile_mask": draw_tile_mask(jax.random.fold_in(arg_keys[5], 71), 0),
    }


def window_stack(blocks, block_count, tile_span):
    return jnp.stack([blocks[offset:offset + block_count] for offset in range(tile_span)], 1)

def attend_grad(query_matrix, key_ext, value_ext, output_gradient, active, logit_scale):
    block_count = query_matrix.shape[0]
    tile_span = active.shape[1]
    query_matrix = query_matrix.astype(jnp.float32)
    output_gradient = output_gradient.astype(jnp.float32)
    windowed_keys = window_stack(key_ext.astype(jnp.float32), block_count, tile_span)
    windowed_values = window_stack(value_ext.astype(jnp.float32), block_count, tile_span)
    attention_logits = jnp.einsum('mip,mejp->meij', query_matrix, windowed_keys) * logit_scale
    masked = jnp.where(active[:, :, None, None], attention_logits, -jnp.inf)
    row_top = lax.optimization_barrier(jnp.max(masked, axis=(1, 3), keepdims=True))
    weights = jnp.exp(masked - row_top)
    denom_sum = lax.optimization_barrier(jnp.sum(weights, axis=(1, 3), keepdims=True))
    prob_f = weights / denom_sum
    backward_probability = lax.optimization_barrier(prob_f.astype(jnp.bfloat16)).astype(jnp.float32)
    probability_gradient = jnp.einsum('mip,mejp->meij', output_gradient, windowed_values)
    row_delta = lax.optimization_barrier(jnp.sum(prob_f * probability_gradient, axis=(1, 3), keepdims=True))
    score_gradient = lax.optimization_barrier((prob_f * (probability_gradient - row_delta)).astype(jnp.bfloat16)).astype(jnp.float32)
    query_gradient_rows = jnp.einsum('luar,lurs->las', score_gradient, windowed_keys) * logit_scale
    windowed_key_gradient = jnp.einsum('gxin,gie->gxne', score_gradient, query_matrix) * logit_scale
    windowed_value_gradient = jnp.einsum('gxin,gie->gxne', backward_probability, output_gradient)
    key_grad = sum((jnp.pad(windowed_key_gradient[:, offset], ((offset, tile_span - 1 - offset), (0, 0), (0, 0))) for offset in range(tile_span)))
    value_grad = sum((jnp.pad(windowed_value_gradient[:, offset], ((offset, tile_span - 1 - offset), (0, 0), (0, 0))) for offset in range(tile_span)))
    return (query_gradient_rows, key_grad, value_grad)

def reference(query, key, value, dout, tile_mask):
    n_tokens, model_width = query.shape
    n_heads = tile_mask.shape[0]
    head_dim = model_width // n_heads
    tile_span = tile_mask.shape[2]
    reach_blocks = tile_span // 2
    all_blocks = n_tokens // BLK
    logit_scale = 1.0 / math.sqrt(head_dim)
    offsets = jnp.arange(tile_span, dtype=jnp.int32) - reach_blocks
    key_block = jnp.arange(all_blocks, dtype=jnp.int32)[:, None] + offsets[None, :]
    key_ok = (key_block >= 0) & (key_block < all_blocks)
    edge_pad = ((reach_blocks, reach_blocks), (0, 0), (0, 0))

    def per_head(head_index):

        def columns(source):
            part_cols = lax.dynamic_slice_in_dim(source, head_index * head_dim, head_dim, 1)
            return part_cols.reshape(all_blocks, BLK, head_dim)
        mask_head = lax.dynamic_index_in_dim(tile_mask, head_index, 0, keepdims=False)
        active = (mask_head != 0) & key_ok
        query_gradient_rows, key_grad, value_grad = attend_grad(columns(query), jnp.pad(columns(key), edge_pad), jnp.pad(columns(value), edge_pad), columns(dout), active, logit_scale)
        inner = slice(reach_blocks, reach_blocks + all_blocks)
        return (query_gradient_rows.astype(jnp.bfloat16).reshape(n_tokens, head_dim), key_grad[inner].astype(jnp.bfloat16).reshape(n_tokens, head_dim), value_grad[inner].astype(jnp.bfloat16).reshape(n_tokens, head_dim))
    grads = lax.map(per_head, jnp.arange(n_heads, dtype=jnp.int32))

    def to_tokens(stacked):
        return jnp.transpose(stacked, (1, 0, 2)).reshape(n_tokens, model_width)
    return (to_tokens(grads[0]), to_tokens(grads[1]), to_tokens(grads[2]))
```

```python
import functools
import math

import jax
import jax.numpy as jnp
from jax import lax
from jax.experimental import pallas as pl
from jax.experimental.pallas import tpu as pltpu
from jax.sharding import PartitionSpec as P

BLK = 128
MESH = pl.DeviceIdType.MESH
AHEAD = 2


def kernel(
    dims,
    bias,
    q_in,
    k_in,
    v_in,
    g_in,
    q_out,
    k_out,
    v_out,
    kv,
    qg,
    acc,
    back,
    rim_put,
    rim_got,
    kv_send,
    kv_recv,
    kv_own,
    qg_send,
    qg_recv,
    qg_own,
    halo_send,
    halo_recv,
    rim_send,
    rim_recv,
    out_send,
    out_recv,
    out_own,
):
    n_ctx, n_uly, tok, hd, slots, span = dims
    rim = span // 2 * BLK
    slab = n_uly * tok
    n_blocks = slab // BLK
    rim_devices = (rim + tok - 1) // tok
    scale = 1.0 / math.sqrt(hd)
    ctx, uly = lax.axis_index("ctx"), lax.axis_index("uly")
    has_prev, has_next = ctx > 0, ctx < n_ctx - 1

    def peer_of(step):
        return lax.rem(uly + step, n_uly)

    def columns(owner, head):
        return pl.ds(pl.multiple_of((owner * slots + head) * hd, hd), hd)

    def own_rows(device):
        return pl.ds(pl.multiple_of(device * tok, tok), tok)

    def ext_rows(device):
        return pl.ds(pl.multiple_of(rim + device * tok, BLK), tok)

    barrier = pltpu.get_barrier_semaphore()

    @pl.loop(1, n_uly)
    def _(step):
        pl.semaphore_signal(
            barrier, inc=1, device_id={"uly": peer_of(step)}, device_id_type=MESH
        )

    @pl.when(has_prev)
    def _():
        pl.semaphore_signal(barrier, inc=1, device_id={"ctx": ctx - 1}, device_id_type=MESH)

    @pl.when(has_next)
    def _():
        pl.semaphore_signal(barrier, inc=1, device_id={"ctx": ctx + 1}, device_id_type=MESH)

    neighbours = has_prev.astype(jnp.int32) + has_next.astype(jnp.int32)
    pl.semaphore_wait(barrier, n_uly - 1 + neighbours)

    def send_head(head):
        for part, source in enumerate((k_in, v_in)):
            pltpu.make_async_copy(
                source.at[:, columns(uly, head)], kv.at[head, part, ext_rows(uly)], kv_own.at[head, part]
            ).start()
        for part, source in enumerate((q_in, g_in)):
            pltpu.make_async_copy(
                source.at[:, columns(uly, head)], qg.at[head, part, own_rows(uly)], qg_own.at[head, part]
            ).start()

        @pl.loop(1, n_uly)
        def _(step):
            peer = peer_of(step)
            for part, source in enumerate((k_in, v_in)):
                pltpu.make_async_remote_copy(
                    src_ref=source.at[:, columns(peer, head)],
                    dst_ref=kv.at[head, part, ext_rows(uly)],
                    send_sem=kv_send.at[head],
                    recv_sem=kv_recv.at[head],
                    device_id={"uly": peer},
                    device_id_type=MESH,
                ).start()
            for part, source in enumerate((q_in, g_in)):
                pltpu.make_async_remote_copy(
                    src_ref=source.at[:, columns(peer, head)],
                    dst_ref=qg.at[head, part, own_rows(uly)],
                    send_sem=qg_send.at[head],
                    recv_sem=qg_recv.at[head],
                    device_id={"uly": peer},
                    device_id_type=MESH,
                ).start()

    def wait_bytes(ref, sem):
        pltpu.make_async_copy(ref, ref, sem).wait()

    def halo_up(head):
        return pltpu.make_async_remote_copy(
            src_ref=kv.at[head, :, pl.ds(slab, rim)],
            dst_ref=kv.at[head, :, pl.ds(0, rim)],
            send_sem=halo_send.at[head, 0],
            recv_sem=halo_recv.at[head, 0],
            device_id={"ctx": ctx + 1},
            device_id_type=MESH,
        )

    def halo_down(head):
        return pltpu.make_async_remote_copy(
            src_ref=kv.at[head, :, pl.ds(rim, rim)],
            dst_ref=kv.at[head, :, pl.ds(rim + slab, rim)],
            send_sem=halo_send.at[head, 1],
            recv_sem=halo_recv.at[head, 1],
            device_id={"ctx": ctx - 1},
            device_id_type=MESH,
        )

    def rim_up(head):
        return pltpu.make_async_remote_copy(
            src_ref=rim_put.at[head, 0],
            dst_ref=rim_got.at[head, 0],
            send_sem=rim_send.at[head, 0],
            recv_sem=rim_recv.at[head, 0],
            device_id={"ctx": ctx + 1},
            device_id_type=MESH,
        )

    def rim_down(head):
        return pltpu.make_async_remote_copy(
            src_ref=rim_put.at[head, 1],
            dst_ref=rim_got.at[head, 1],
            send_sem=rim_send.at[head, 1],
            recv_sem=rim_recv.at[head, 1],
            device_id={"ctx": ctx - 1},
            device_id_type=MESH,
        )

    def send_back(head, peer, parts):
        for part, target in enumerate((q_out, k_out, v_out)):
            if part in parts:
                pltpu.make_async_remote_copy(
                    src_ref=back.at[head, part, own_rows(peer)],
                    dst_ref=target.at[:, columns(uly, head)],
                    send_sem=out_send.at[part],
                    recv_sem=out_recv.at[part],
                    device_id={"uly": peer},
                    device_id_type=MESH,
                ).start()

    def keep(head, parts):
        for part, target in enumerate((q_out, k_out, v_out)):
            if part in parts:
                pltpu.make_async_copy(
                    back.at[head, part, own_rows(uly)],
                    target.at[:, columns(uly, head)],
                    out_own.at[part],
                ).start()

    def is_rim(device):
        return (device < rim_devices) | (device >= n_uly - rim_devices)

    def attend(head):
        acc[...] = jnp.zeros_like(acc)

        @pl.loop(0, n_blocks)
        def _(block):
            row = pl.multiple_of(block * BLK, BLK)
            k_win = kv[head, 0, pl.ds(row, span * BLK), :]
            v_win = kv[head, 1, pl.ds(row, span * BLK), :]
            q = qg[head, 0, pl.ds(row, BLK), :]
            g = qg[head, 1, pl.ds(row, BLK), :]
            nt = (((1,), (1,)), ((), ()))
            logits = lax.dot_general(k_win, q, nt, preferred_element_type=jnp.float32)
            place = (head * n_blocks + block) * span
            logits = jnp.concatenate(
                [logits[o * BLK : (o + 1) * BLK] + bias[place + o] for o in range(span)], axis=0
            )
            top = jnp.max(logits, axis=0, keepdims=True)
            weights = jnp.exp((logits - top) * scale)
            prob = weights * (1.0 / jnp.sum(weights, axis=0, keepdims=True))
            dprob = lax.dot_general(v_win, g, nt, preferred_element_type=jnp.float32)
            delta = jnp.sum(prob * dprob, axis=0, keepdims=True)
            dscore = (prob * (dprob - delta)).astype(jnp.bfloat16)
            prob_b = prob.astype(jnp.bfloat16)
            acc[0, pl.ds(row, span * BLK), :] += jnp.dot(
                dscore, q, preferred_element_type=jnp.float32
            )
            acc[1, pl.ds(row, span * BLK), :] += jnp.dot(
                prob_b, g, preferred_element_type=jnp.float32
            )
            dq = lax.dot_general(
                dscore, k_win, (((0,), (0,)), ((), ())), preferred_element_type=jnp.float32
            )
            back[head, 0, pl.ds(row, BLK), :] = (dq * scale).astype(jnp.bfloat16)

    @pl.when(jnp.logical_not(has_prev))
    def _():
        kv[:, :, :rim, :] = jnp.zeros((slots, 2, rim, hd), jnp.bfloat16)

    @pl.when(jnp.logical_not(has_next))
    def _():
        kv[:, :, rim + slab :, :] = jnp.zeros((slots, 2, rim, hd), jnp.bfloat16)

    @pl.loop(0, min(AHEAD, slots))
    def _(head):
        send_head(head)

    @pl.loop(0, slots)
    def _(head):
        @pl.when(head + AHEAD < slots)
        def _():
            send_head(head + AHEAD)

        for part in range(2):
            wait_bytes(kv.at[head, part, pl.ds(0, tok)], kv_own.at[head, part])
        wait_bytes(kv.at[head, :, pl.ds(0, (n_uly - 1) * tok)], kv_recv.at[head])

        @pl.when(has_next)
        def _():
            halo_up(head).start()

        @pl.when(has_prev)
        def _():
            halo_down(head).start()

        for part in range(2):
            wait_bytes(qg.at[head, part, pl.ds(0, tok)], qg_own.at[head, part])
        wait_bytes(qg.at[head, :, pl.ds(0, (n_uly - 1) * tok)], qg_recv.at[head])

        @pl.when(has_prev)
        def _():
            halo_up(head).wait_recv()

        @pl.when(has_next)
        def _():
            halo_down(head).wait_recv()

        attend(head)
        scales = (scale, 1.0)

        for part in range(2):
            rim_put[head, 0, part] = (acc[part, rim + slab :, :] * scales[part]).astype(jnp.bfloat16)
            rim_put[head, 1, part] = (acc[part, :rim, :] * scales[part]).astype(jnp.bfloat16)

        @pl.when(has_next)
        def _():
            rim_up(head).start()

        @pl.when(has_prev)
        def _():
            rim_down(head).start()

        if slab > 2 * rim:
            for part in range(2):
                back[head, 1 + part, rim : slab - rim, :] = (
                    acc[part, 2 * rim : slab, :] * scales[part]
                ).astype(jnp.bfloat16)

        @pl.loop(1, n_uly)
        def _(step):
            peer = peer_of(step)
            send_back(head, peer, (0,))

            @pl.when(jnp.logical_not(is_rim(peer)))
            def _():
                send_back(head, peer, (1, 2))

        keep(head, (0,))

        for part in range(2):
            first = acc[part, rim : 2 * rim, :] * scales[part]
            last = acc[part, slab : slab + rim, :] * scales[part]
            acc[part, rim : 2 * rim, :] = first
            acc[part, slab : slab + rim, :] = last

        @pl.when(has_prev)
        def _():
            rim_up(head).wait_recv()
            for part in range(2):
                acc[part, rim : 2 * rim, :] += rim_got[head, 0, part].astype(jnp.float32)

        @pl.when(has_next)
        def _():
            rim_down(head).wait_recv()
            for part in range(2):
                acc[part, slab : slab + rim, :] += rim_got[head, 1, part].astype(jnp.float32)

        for part in range(2):
            back[head, 1 + part, :rim, :] = acc[part, rim : 2 * rim, :].astype(jnp.bfloat16)
            back[head, 1 + part, slab - rim :, :] = acc[part, slab : slab + rim, :].astype(
                jnp.bfloat16
            )
        keep(head, (1, 2))

        @pl.loop(1, n_uly)
        def _(step):
            peer = peer_of(step)

            @pl.when(is_rim(peer))
            def _():
                send_back(head, peer, (1, 2))

    @pl.loop(0, slots)
    def _(head):
        wait_bytes(kv.at[head, :, pl.ds(0, (n_uly - 1) * tok)], kv_send.at[head])
        wait_bytes(qg.at[head, :, pl.ds(0, (n_uly - 1) * tok)], qg_send.at[head])

        @pl.when(has_next)
        def _():
            halo_up(head).wait_send()
            rim_up(head).wait_send()

        @pl.when(has_prev)
        def _():
            halo_down(head).wait_send()
            rim_down(head).wait_send()

    for part, target in enumerate((q_out, k_out, v_out)):
        wait_bytes(target.at[:, pl.ds(0, slots * hd)], out_own.at[part])
        wait_bytes(target.at[:, pl.ds(0, (n_uly - 1) * slots * hd)], out_send.at[part])
        wait_bytes(target.at[:, pl.ds(0, (n_uly - 1) * slots * hd)], out_recv.at[part])


def shards(query, key, value, dout, tile_mask):
    n_ctx, n_uly = lax.axis_size("ctx"), lax.axis_size("uly")
    tok, width = query.shape
    n_heads, all_blocks, span = tile_mask.shape
    hd = width // n_heads
    reach = span // 2
    rim = reach * BLK
    slab = tok * n_uly
    n_blocks = slab // BLK
    slots = (n_heads + n_uly - 1) // n_uly
    extra = slots * n_uly - n_heads
    full = slots * n_uly * hd

    mask = jnp.pad(tile_mask, ((0, extra), (0, 0), (0, 0)))
    first_block = lax.axis_index("ctx") * n_blocks
    mask = lax.dynamic_slice(
        mask, (lax.axis_index("uly") * slots, first_block, 0), (slots, n_blocks, span)
    )
    offsets = jnp.arange(span, dtype=jnp.int32) - reach
    key_block = first_block + jnp.arange(n_blocks, dtype=jnp.int32)[:, None] + offsets[None, :]
    key_ok = (key_block >= 0) & (key_block < all_blocks)
    active = ((mask != 0) & key_ok[None]) | (offsets == 0)
    bias = jnp.where(active, 0.0, -jnp.inf).astype(jnp.float32).reshape(-1)

    arrays = (query, key, value, dout)
    if extra:
        arrays = tuple(jnp.pad(a, ((0, 0), (0, extra * hd))) for a in arrays)
    dims = (n_ctx, n_uly, tok, hd, slots, span)
    dma = pltpu.SemaphoreType.DMA
    anywhere = pl.BlockSpec(memory_space=pl.ANY)
    outs = pl.pallas_call(
        functools.partial(kernel, dims),
        out_shape=[jax.ShapeDtypeStruct((tok, full), jnp.bfloat16)] * 3,
        in_specs=[pl.BlockSpec(memory_space=pltpu.SMEM)] + [anywhere] * 4,
        out_specs=[anywhere] * 3,
        scratch_shapes=[
            pltpu.VMEM((slots, 2, slab + 2 * rim, hd), jnp.bfloat16),
            pltpu.VMEM((slots, 2, slab, hd), jnp.bfloat16),
            pltpu.VMEM((2, slab + 2 * rim, hd), jnp.float32),
            pltpu.VMEM((slots, 3, slab, hd), jnp.bfloat16),
            pltpu.VMEM((slots, 2, 2, rim, hd), jnp.bfloat16),
            pltpu.VMEM((slots, 2, 2, rim, hd), jnp.bfloat16),
            dma((slots,)),
            dma((slots,)),
            dma((slots, 2)),
            dma((slots,)),
            dma((slots,)),
            dma((slots, 2)),
            dma((slots, 2)),
            dma((slots, 2)),
            dma((slots, 2)),
            dma((slots, 2)),
            dma((3,)),
            dma((3,)),
            dma((3,)),
        ],
        compiler_params=pltpu.CompilerParams(
            collective_id=0, has_side_effects=True, vmem_limit_bytes=48 * 2**20
        ),
        cost_estimate=pl.CostEstimate(
            flops=10 * slots * slab * span * BLK * hd,
            bytes_accessed=14 * tok * full,
            transcendentals=slots * slab * span * BLK,
        ),
        name="tile_attention_grad",
    )(bias, *arrays)
    return tuple(o[:, :width] for o in outs)


def solution(mesh):
    rows = P(("ctx", "uly"), None)
    return jax.shard_map(
        shards,
        mesh=mesh,
        in_specs=(rows, rows, rows, rows, P()),
        out_specs=(rows, rows, rows),
        check_vma=False,
    )
```

```python
import functools
import math

import jax
import jax.numpy as jnp
from jax import lax
from jax.experimental import pallas as pl
from jax.experimental.pallas import tpu as pltpu
from jax.sharding import PartitionSpec as P

BLK = 128
MESH = pl.DeviceIdType.MESH
NEVER = -1e30
AHEAD = 3
LAG = 2


def kernel(
    dims,
    bias,
    q_in,
    k_in,
    v_in,
    g_in,
    q_out,
    k_out,
    v_out,
    kv,
    qg,
    part_own,
    part_put,
    part_got,
    stat_own,
    stat_got,
    dq_own,
    dq_put,
    dq_got,
    back,
    in_send,
    in_recv,
    in_own,
    qg_send,
    qg_recv,
    part_send,
    part_recv,
    stat_send,
    stat_recv,
    dq_send,
    dq_recv,
    out_send,
    out_recv,
    out_own,
):
    n_ctx, n_uly, tok, hd, slots, group = dims
    rows = group * tok
    nb = rows // BLK
    n_devices = n_ctx * n_uly
    scale = 1.0 / math.sqrt(hd)
    uly = lax.axis_index("uly")
    place = lax.axis_index("ctx") * n_uly + uly
    member = lax.rem(uly, group)
    chunk_start = uly - member
    has_prev = place >= group
    has_next = place < n_devices - group

    def device(index):
        return {"ctx": lax.div(index, n_uly), "uly": lax.rem(index, n_uly)}

    next_id = device(lax.rem(place + group, n_devices))
    prev_id = device(lax.rem(place + n_devices - group, n_devices))

    def columns(owner, head):
        return pl.ds(pl.multiple_of((owner * slots + head) * hd, hd), hd)

    def token_rows(owner):
        return pl.ds(pl.multiple_of(owner * tok, tok), tok)

    def other(step):
        return lax.rem(member + step, group)

    barrier = pltpu.get_barrier_semaphore()
    for step in range(1, group):
        pl.semaphore_signal(
            barrier, inc=1, device_id={"uly": chunk_start + other(step)}, device_id_type=MESH
        )

    @pl.when(has_prev)
    def _():
        pl.semaphore_signal(barrier, inc=1, device_id=prev_id, device_id_type=MESH)

    @pl.when(has_next)
    def _():
        pl.semaphore_signal(barrier, inc=1, device_id=next_id, device_id_type=MESH)

    neighbours = has_prev.astype(jnp.int32) + has_next.astype(jnp.int32)
    pl.semaphore_wait(barrier, group - 1 + neighbours)

    def wait_bytes(ref, sem):
        pltpu.make_async_copy(ref, ref, sem).wait()

    def landing(head, part, owner):
        return (
            kv.at[head, part, token_rows(owner)]
            if part < 2
            else qg.at[head, 1, part - 2, token_rows(owner)]
        )

    def send_in(head):
        for part, source in enumerate((k_in, v_in, q_in, g_in)):
            pltpu.make_async_copy(
                source.at[:, columns(member, head)],
                landing(head, part, member),
                in_own.at[head, part],
            ).start()
            for step in range(1, group):
                pltpu.make_async_remote_copy(
                    src_ref=source.at[:, columns(other(step), head)],
                    dst_ref=landing(head, part, member),
                    send_sem=in_send.at[part],
                    recv_sem=in_recv.at[head, part],
                    device_id={"uly": chunk_start + other(step)},
                    device_id_type=MESH,
                ).start()

    def to_both(sources, targets, send_sem, recv_sem, head):
        for side, there, exists in ((0, next_id, has_next), (1, prev_id, has_prev)):

            @pl.when(exists)
            def _():
                pltpu.make_async_remote_copy(
                    src_ref=sources[side],
                    dst_ref=targets[side],
                    send_sem=send_sem.at[side],
                    recv_sem=recv_sem.at[head, side],
                    device_id=there,
                    device_id_type=MESH,
                ).start()

    def from_both(targets, recv_sem, head):
        for side, exists in ((0, has_prev), (1, has_next)):

            @pl.when(exists)
            def _():
                wait_bytes(targets[side], recv_sem.at[head, side])

    def sides(ref, head):
        return (ref.at[head, 0], ref.at[head, 1])

    def outer_qg(head):
        return (qg.at[head, 0], qg.at[head, 2])

    def forward(head):
        for part in range(4):
            ref = kv.at[head, part] if part < 2 else qg.at[head, 1, part - 2]
            wait_bytes(ref.at[pl.ds(0, tok)], in_own.at[head, part])
            if group > 1:
                wait_bytes(ref.at[pl.ds(0, (group - 1) * tok)], in_recv.at[head, part])
        to_both((qg.at[head, 1], qg.at[head, 1]), outer_qg(head), qg_send, qg_recv, head)

    def logits_of(head, position):
        nt = (((1,), (1,)), ((), ()))
        k, v = kv[head, 0], kv[head, 1]
        q, g = qg[head, position, 0], qg[head, position, 1]
        raw = lax.dot_general(k, q, nt, preferred_element_type=jnp.float32)
        first = (head * 3 + position) * nb * nb
        raw = jnp.concatenate(
            [
                jnp.concatenate(
                    [
                        raw[i * BLK : (i + 1) * BLK, j * BLK : (j + 1) * BLK]
                        + bias[first + j * nb + i]
                        for j in range(nb)
                    ],
                    axis=1,
                )
                for i in range(nb)
            ],
            axis=0,
        )
        dprob = lax.dot_general(v, g, nt, preferred_element_type=jnp.float32)
        return k, q, g, raw, dprob

    def packed(values):
        pieces = [v[:, j * BLK : (j + 1) * BLK] for v in values for j in range(nb)]
        pad = part_own.shape[1] - len(pieces)
        if pad:
            pieces.append(jnp.zeros((pad, BLK), jnp.float32))
        return jnp.concatenate(pieces, axis=0)

    def unpacked(tile, which):
        return jnp.concatenate(
            [tile[which * nb + j : which * nb + j + 1] for j in range(nb)], axis=1
        )

    def partial_stats(head):
        from_both(outer_qg(head), qg_recv, head)
        for position in range(3):
            _, _, _, raw, dprob = logits_of(head, position)
            top = jnp.max(raw, axis=0, keepdims=True)
            weights = jnp.exp((raw - top) * scale)
            total = jnp.sum(weights, axis=0, keepdims=True)
            mixed = jnp.sum(weights * dprob, axis=0, keepdims=True)
            tile = packed((top, total, mixed))
            if position == 1:
                part_own[head] = tile
            else:
                part_put[head, 0 if position == 2 else 1] = tile
        to_both(sides(part_put, head), sides(part_got, head), part_send, part_recv, head)

    def final_stats(head):
        from_both(sides(part_got, head), part_recv, head)
        tiles = (part_own[head], part_got[head, 0], part_got[head, 1])
        tops = [t[:nb] for t in tiles]
        top = jnp.maximum(jnp.maximum(tops[0], tops[1]), tops[2])
        factors = [jnp.exp((t - top) * scale) for t in tops]
        total = sum(t[nb : 2 * nb] * f for t, f in zip(tiles, factors))
        mixed = sum(t[2 * nb : 3 * nb] * f for t, f in zip(tiles, factors))
        inverse = 1.0 / total
        pieces = [top, inverse, mixed * inverse]
        pad = part_own.shape[1] - 3 * nb
        if pad:
            pieces.append(jnp.zeros((pad, BLK), jnp.float32))
        stat_own[head] = jnp.concatenate(pieces, axis=0)
        own = (stat_own.at[head], stat_own.at[head])
        to_both(own, sides(stat_got, head), stat_send, stat_recv, head)

    def gather_out(head, parts):
        for part, target in enumerate((q_out, k_out, v_out)):
            if part not in parts:
                continue
            pltpu.make_async_copy(
                back.at[head, part, token_rows(member)],
                target.at[:, columns(member, head)],
                out_own.at[part],
            ).start()
            for step in range(1, group):
                pltpu.make_async_remote_copy(
                    src_ref=back.at[head, part, token_rows(other(step))],
                    dst_ref=target.at[:, columns(member, head)],
                    send_sem=out_send.at[part],
                    recv_sem=out_recv.at[part],
                    device_id={"uly": chunk_start + other(step)},
                    device_id_type=MESH,
                ).start()

    def gradients(head):
        from_both(sides(stat_got, head), stat_recv, head)
        dk = jnp.zeros((rows, hd), jnp.float32)
        dv = jnp.zeros((rows, hd), jnp.float32)
        for position in range(3):
            tile = stat_own[head] if position == 1 else stat_got[head, position // 2]
            k, q, g, raw, dprob = logits_of(head, position)
            prob = jnp.exp((raw - unpacked(tile, 0)) * scale) * unpacked(tile, 1)
            dscore = (prob * (dprob - unpacked(tile, 2))).astype(jnp.bfloat16)
            dk += jnp.dot(dscore, q, preferred_element_type=jnp.float32)
            dv += jnp.dot(prob.astype(jnp.bfloat16), g, preferred_element_type=jnp.float32)
            tn = (((0,), (0,)), ((), ()))
            dq = lax.dot_general(dscore, k, tn, preferred_element_type=jnp.float32) * scale
            if position == 1:
                dq_own[head] = dq
            else:
                dq_put[head, 0 if position == 2 else 1] = dq.astype(jnp.bfloat16)
        to_both(sides(dq_put, head), sides(dq_got, head), dq_send, dq_recv, head)
        back[head, 1] = (dk * scale).astype(jnp.bfloat16)
        back[head, 2] = dv.astype(jnp.bfloat16)
        gather_out(head, (1, 2))

    def finish(head):
        from_both(sides(dq_got, head), dq_recv, head)
        dq = dq_own[head] + dq_got[head, 0].astype(jnp.float32)
        back[head, 0] = (dq + dq_got[head, 1].astype(jnp.float32)).astype(jnp.bfloat16)
        gather_out(head, (0,))

    for side, exists in ((0, has_prev), (1, has_next)):

        @pl.when(jnp.logical_not(exists))
        def _():
            @pl.loop(0, slots)
            def _(head):
                qg[head, 2 * side] = jnp.zeros((2, rows, hd), jnp.bfloat16)
                part_got[head, side] = jnp.full(part_own.shape[1:], NEVER, jnp.float32)
                stat_got[head, side] = jnp.zeros(part_own.shape[1:], jnp.float32)
                dq_got[head, side] = jnp.zeros((rows, hd), jnp.bfloat16)

    @pl.loop(0, min(AHEAD, slots))
    def _(head):
        send_in(head)

    stages = ((0, forward), (LAG, partial_stats), (LAG + 1, final_stats), (LAG + 2, gradients), (LAG + 3, finish))

    @pl.loop(0, slots + LAG + 3)
    def _(turn):
        @pl.when(turn + AHEAD < slots)
        def _():
            send_in(turn + AHEAD)

        for lag, stage in stages:

            @pl.when((turn >= lag) & (turn < slots + lag))
            def _():
                stage(turn - lag)

    far = (group - 1) * slots * hd
    for part, target in enumerate((q_out, k_out, v_out)):
        wait_bytes(target.at[:, pl.ds(0, slots * hd)], out_own.at[part])
        if group > 1:
            wait_bytes(target.at[:, pl.ds(0, far)], out_send.at[part])
            wait_bytes(target.at[:, pl.ds(0, far)], out_recv.at[part])
    if group > 1:
        for part in range(4):
            wait_bytes(k_in.at[:, pl.ds(0, far)], in_send.at[part])
    for side, exists in ((0, has_next), (1, has_prev)):

        @pl.when(exists)
        def _():
            wait_bytes(qg.at[:, 1], qg_send.at[side])
            wait_bytes(part_put.at[:, side], part_send.at[side])
            wait_bytes(stat_own, stat_send.at[side])
            wait_bytes(dq_put.at[:, side], dq_send.at[side])


def shards(query, key, value, dout, tile_mask):
    n_ctx, n_uly = lax.axis_size("ctx"), lax.axis_size("uly")
    tok, width = query.shape
    n_heads, _, span = tile_mask.shape
    hd = width // n_heads
    reach = span // 2
    group = reach * BLK // tok
    rows = group * tok
    nb = rows // BLK
    slots = (n_heads + group - 1) // group
    extra = slots * group - n_heads
    full = slots * group * hd

    place = lax.axis_index("ctx") * n_uly + lax.axis_index("uly")
    chunk, member = place // group, place % group
    mask = jnp.pad(tile_mask, ((0, extra), (nb, nb), (0, 0)))
    mask = lax.dynamic_slice(mask, (member * slots, chunk * nb, 0), (slots, 3 * nb, span))
    none = jnp.zeros((slots,), tile_mask.dtype)
    pairs = [
        mask[:, j, nb + i - j + reach] if 0 <= nb + i - j + reach < span else none
        for j in range(3 * nb)
        for i in range(nb)
    ]
    bias = jnp.where(jnp.stack(pairs, 1) != 0, 0.0, NEVER).astype(jnp.float32).reshape(-1)

    arrays = (query, key, value, dout)
    if extra:
        arrays = tuple(jnp.pad(a, ((0, 0), (0, extra * hd))) for a in arrays)
    dims = (n_ctx, n_uly, tok, hd, slots, group)
    stat_rows = (3 * nb + 7) // 8 * 8
    dma = pltpu.SemaphoreType.DMA
    anywhere = pl.BlockSpec(memory_space=pl.ANY)
    outs = pl.pallas_call(
        functools.partial(kernel, dims),
        out_shape=[jax.ShapeDtypeStruct((tok, full), jnp.bfloat16)] * 3,
        in_specs=[pl.BlockSpec(memory_space=pltpu.SMEM)] + [anywhere] * 4,
        out_specs=[anywhere] * 3,
        scratch_shapes=[
            pltpu.VMEM((slots, 2, rows, hd), jnp.bfloat16),
            pltpu.VMEM((slots, 3, 2, rows, hd), jnp.bfloat16),
            pltpu.VMEM((slots, stat_rows, BLK), jnp.float32),
            pltpu.VMEM((slots, 2, stat_rows, BLK), jnp.float32),
            pltpu.VMEM((slots, 2, stat_rows, BLK), jnp.float32),
            pltpu.VMEM((slots, stat_rows, BLK), jnp.float32),
            pltpu.VMEM((slots, 2, stat_rows, BLK), jnp.float32),
            pltpu.VMEM((slots, rows, hd), jnp.float32),
            pltpu.VMEM((slots, 2, rows, hd), jnp.bfloat16),
            pltpu.VMEM((slots, 2, rows, hd), jnp.bfloat16),
            pltpu.VMEM((slots, 3, rows, hd), jnp.bfloat16),
            dma((4,)),
            dma((slots, 4)),
            dma((slots, 4)),
            dma((2,)),
            dma((slots, 2)),
            dma((2,)),
            dma((slots, 2)),
            dma((2,)),
            dma((slots, 2)),
            dma((2,)),
            dma((slots, 2)),
            dma((3,)),
            dma((3,)),
            dma((3,)),
        ],
        compiler_params=pltpu.CompilerParams(
            collective_id=0, has_side_effects=True, vmem_limit_bytes=48 * 2**20
        ),
        cost_estimate=pl.CostEstimate(
            flops=42 * slots * rows * rows * hd,
            bytes_accessed=14 * tok * full,
            transcendentals=6 * slots * rows * rows,
        ),
        name="tile_attention_grad",
    )(bias, *arrays)
    return tuple(o[:, :width] for o in outs)


def solution(mesh):
    rows = P(("ctx", "uly"), None)
    return jax.shard_map(
        shards,
        mesh=mesh,
        in_specs=(rows, rows, rows, rows, P()),
        out_specs=(rows, rows, rows),
        check_vma=False,
    )
```

```python
import functools
import math

import jax
import jax.numpy as jnp
from jax import lax
from jax.experimental import pallas as pl
from jax.experimental.pallas import tpu as pltpu
from jax.sharding import PartitionSpec as P

BLK = 128
MESH = pl.DeviceIdType.MESH
NEVER = -1e30
AHEAD = 3
LAG = 2


def kernel(
    dims,
    bias,
    q_in,
    k_in,
    v_in,
    g_in,
    q_out,
    k_out,
    v_out,
    kv,
    qg,
    part_own,
    part_put,
    part_got,
    stat_own,
    stat_got,
    dq_own,
    dq_put,
    dq_got,
    back,
    in_send,
    in_recv,
    in_own,
    qg_send,
    qg_recv,
    part_send,
    part_recv,
    stat_send,
    stat_recv,
    dq_send,
    dq_recv,
    out_send,
    out_recv,
    out_own,
):
    n_ctx, n_uly, tok, hd, slots, group = dims
    rows = group * tok
    nb = rows // BLK
    n_devices = n_ctx * n_uly
    scale = 1.0 / math.sqrt(hd)
    uly = lax.axis_index("uly")
    place = lax.axis_index("ctx") * n_uly + uly
    member = lax.rem(uly, group)
    chunk_start = uly - member
    has_prev = place >= group
    has_next = place < n_devices - group

    def device(index):
        return {"ctx": lax.div(index, n_uly), "uly": lax.rem(index, n_uly)}

    next_id = device(lax.rem(place + group, n_devices))
    prev_id = device(lax.rem(place + n_devices - group, n_devices))

    def columns(owner, head):
        return pl.ds(pl.multiple_of((owner * slots + head) * hd, hd), hd)

    def token_rows(owner):
        return pl.ds(pl.multiple_of(owner * tok, tok), tok)

    def other(step):
        return lax.rem(member + step, group)

    barrier = pltpu.get_barrier_semaphore()
    for step in range(1, group):
        pl.semaphore_signal(
            barrier, inc=1, device_id={"uly": chunk_start + other(step)}, device_id_type=MESH
        )

    @pl.when(has_prev)
    def _():
        pl.semaphore_signal(barrier, inc=1, device_id=prev_id, device_id_type=MESH)

    @pl.when(has_next)
    def _():
        pl.semaphore_signal(barrier, inc=1, device_id=next_id, device_id_type=MESH)

    neighbours = has_prev.astype(jnp.int32) + has_next.astype(jnp.int32)
    pl.semaphore_wait(barrier, group - 1 + neighbours)

    def wait_bytes(ref, sem):
        pltpu.make_async_copy(ref, ref, sem).wait()

    def landing(head, part, owner):
        return (
            kv.at[head, part, token_rows(owner)]
            if part < 2
            else qg.at[head, 1, part - 2, token_rows(owner)]
        )

    def send_in(head):
        for part, source in enumerate((k_in, v_in, q_in, g_in)):
            pltpu.make_async_copy(
                source.at[:, columns(member, head)],
                landing(head, part, member),
                in_own.at[head, part],
            ).start()
            for step in range(1, group):
                pltpu.make_async_remote_copy(
                    src_ref=source.at[:, columns(other(step), head)],
                    dst_ref=landing(head, part, member),
                    send_sem=in_send.at[part],
                    recv_sem=in_recv.at[head, part],
                    device_id={"uly": chunk_start + other(step)},
                    device_id_type=MESH,
                ).start()

    def to_both(sources, targets, send_sem, recv_sem, head):
        for side, there, exists in ((0, next_id, has_next), (1, prev_id, has_prev)):

            @pl.when(exists)
            def _():
                pltpu.make_async_remote_copy(
                    src_ref=sources[side],
                    dst_ref=targets[side],
                    send_sem=send_sem.at[side],
                    recv_sem=recv_sem.at[head, side],
                    device_id=there,
                    device_id_type=MESH,
                ).start()

    def from_both(targets, recv_sem, head):
        for side, exists in ((0, has_prev), (1, has_next)):

            @pl.when(exists)
            def _():
                wait_bytes(targets[side], recv_sem.at[head, side])

    def stat_sides(ref, head):
        return (ref.at[head, 0, pl.ds(0, 3 * nb)], ref.at[head, 1, pl.ds(0, 3 * nb)])

    def sides(ref, head):
        return (ref.at[head, 0], ref.at[head, 1])

    def outer_qg(head):
        return (qg.at[head, 0], qg.at[head, 2])

    def forward(head):
        for part in range(4):
            ref = kv.at[head, part] if part < 2 else qg.at[head, 1, part - 2]
            wait_bytes(ref.at[pl.ds(0, tok)], in_own.at[head, part])
            if group > 1:
                wait_bytes(ref.at[pl.ds(0, (group - 1) * tok)], in_recv.at[head, part])
        to_both((qg.at[head, 1], qg.at[head, 1]), outer_qg(head), qg_send, qg_recv, head)

    def logits_of(head, position):
        nt = (((1,), (1,)), ((), ()))
        k, v = kv[head, 0], kv[head, 1]
        q, g = qg[head, position, 0], qg[head, position, 1]
        raw = lax.dot_general(k, q, nt, preferred_element_type=jnp.float32)
        first = (head * 3 + position) * nb * nb
        raw = jnp.concatenate(
            [
                jnp.concatenate(
                    [
                        raw[i * BLK : (i + 1) * BLK, j * BLK : (j + 1) * BLK]
                        + bias[first + j * nb + i]
                        for j in range(nb)
                    ],
                    axis=1,
                )
                for i in range(nb)
            ],
            axis=0,
        )
        dprob = lax.dot_general(v, g, nt, preferred_element_type=jnp.float32)
        return k, q, g, raw, dprob

    def packed(values):
        pieces = [v[:, j * BLK : (j + 1) * BLK] for v in values for j in range(nb)]
        pad = part_own.shape[1] - len(pieces)
        if pad:
            pieces.append(jnp.zeros((pad, BLK), jnp.float32))
        return jnp.concatenate(pieces, axis=0)

    def unpacked(tile, which):
        return jnp.concatenate(
            [tile[which * nb + j : which * nb + j + 1] for j in range(nb)], axis=1
        )

    def partial_stats(head):
        from_both(outer_qg(head), qg_recv, head)
        for position in range(3):
            _, _, _, raw, dprob = logits_of(head, position)
            top = jnp.max(raw, axis=0, keepdims=True)
            weights = jnp.exp((raw - top) * scale)
            total = jnp.sum(weights, axis=0, keepdims=True)
            mixed = jnp.sum(weights * dprob, axis=0, keepdims=True)
            tile = packed((top, total, mixed))
            if position == 1:
                part_own[head] = tile
            else:
                part_put[head, 0 if position == 2 else 1] = tile
        to_both(stat_sides(part_put, head), stat_sides(part_got, head), part_send, part_recv, head)

    def final_stats(head):
        from_both(stat_sides(part_got, head), part_recv, head)
        tiles = (part_own[head], part_got[head, 0], part_got[head, 1])
        tops = [t[:nb] for t in tiles]
        top = jnp.maximum(jnp.maximum(tops[0], tops[1]), tops[2])
        factors = [jnp.exp((t - top) * scale) for t in tops]
        total = sum(t[nb : 2 * nb] * f for t, f in zip(tiles, factors))
        mixed = sum(t[2 * nb : 3 * nb] * f for t, f in zip(tiles, factors))
        inverse = 1.0 / total
        pieces = [top, inverse, mixed * inverse]
        pad = part_own.shape[1] - 3 * nb
        if pad:
            pieces.append(jnp.zeros((pad, BLK), jnp.float32))
        stat_own[head] = jnp.concatenate(pieces, axis=0)
        own = (stat_own.at[head, pl.ds(0, 3 * nb)],) * 2
        to_both(own, stat_sides(stat_got, head), stat_send, stat_recv, head)

    def gather_out(head, parts):
        for part, target in enumerate((q_out, k_out, v_out)):
            if part not in parts:
                continue
            pltpu.make_async_copy(
                back.at[head, part, token_rows(member)],
                target.at[:, columns(member, head)],
                out_own.at[part],
            ).start()
            for step in range(1, group):
                pltpu.make_async_remote_copy(
                    src_ref=back.at[head, part, token_rows(other(step))],
                    dst_ref=target.at[:, columns(member, head)],
                    send_sem=out_send.at[part],
                    recv_sem=out_recv.at[part],
                    device_id={"uly": chunk_start + other(step)},
                    device_id_type=MESH,
                ).start()

    def gradients(head):
        from_both(stat_sides(stat_got, head), stat_recv, head)
        dk = jnp.zeros((rows, hd), jnp.float32)
        dv = jnp.zeros((rows, hd), jnp.float32)
        for position in range(3):
            tile = stat_own[head] if position == 1 else stat_got[head, position // 2]
            k, q, g, raw, dprob = logits_of(head, position)
            prob = jnp.exp((raw - unpacked(tile, 0)) * scale) * unpacked(tile, 1)
            dscore = (prob * (dprob - unpacked(tile, 2))).astype(jnp.bfloat16)
            dk += jnp.dot(dscore, q, preferred_element_type=jnp.float32)
            dv += jnp.dot(prob.astype(jnp.bfloat16), g, preferred_element_type=jnp.float32)
            tn = (((0,), (0,)), ((), ()))
            dq = lax.dot_general(dscore, k, tn, preferred_element_type=jnp.float32) * scale
            if position == 1:
                dq_own[head] = dq
            else:
                dq_put[head, 0 if position == 2 else 1] = dq.astype(jnp.bfloat16)
        to_both(sides(dq_put, head), sides(dq_got, head), dq_send, dq_recv, head)
        back[head, 1] = (dk * scale).astype(jnp.bfloat16)
        back[head, 2] = dv.astype(jnp.bfloat16)
        gather_out(head, (1, 2))

    def finish(head):
        from_both(sides(dq_got, head), dq_recv, head)
        dq = dq_own[head] + dq_got[head, 0].astype(jnp.float32)
        back[head, 0] = (dq + dq_got[head, 1].astype(jnp.float32)).astype(jnp.bfloat16)
        gather_out(head, (0,))

    for side, exists in ((0, has_prev), (1, has_next)):

        @pl.when(jnp.logical_not(exists))
        def _():
            @pl.loop(0, slots)
            def _(head):
                qg[head, 2 * side] = jnp.zeros((2, rows, hd), jnp.bfloat16)
                part_got[head, side] = jnp.full(part_own.shape[1:], NEVER, jnp.float32)
                stat_got[head, side] = jnp.zeros(part_own.shape[1:], jnp.float32)
                dq_got[head, side] = jnp.zeros((rows, hd), jnp.bfloat16)

    @pl.loop(0, min(AHEAD, slots))
    def _(head):
        send_in(head)

    stages = ((0, forward), (LAG, partial_stats), (LAG + 1, final_stats), (LAG + 2, gradients), (LAG + 3, finish))

    @pl.loop(0, slots + LAG + 3)
    def _(turn):
        @pl.when(turn + AHEAD < slots)
        def _():
            send_in(turn + AHEAD)

        for lag, stage in stages:

            @pl.when((turn >= lag) & (turn < slots + lag))
            def _():
                stage(turn - lag)

    far = (group - 1) * slots * hd
    for part, target in enumerate((q_out, k_out, v_out)):
        wait_bytes(target.at[:, pl.ds(0, slots * hd)], out_own.at[part])
        if group > 1:
            wait_bytes(target.at[:, pl.ds(0, far)], out_send.at[part])
            wait_bytes(target.at[:, pl.ds(0, far)], out_recv.at[part])
    if group > 1:
        for part in range(4):
            wait_bytes(k_in.at[:, pl.ds(0, far)], in_send.at[part])
    for side, exists in ((0, has_next), (1, has_prev)):

        @pl.when(exists)
        def _():
            wait_bytes(qg.at[:, 1], qg_send.at[side])
            wait_bytes(part_put.at[:, side, pl.ds(0, 3 * nb)], part_send.at[side])
            wait_bytes(stat_own.at[:, pl.ds(0, 3 * nb)], stat_send.at[side])
            wait_bytes(dq_put.at[:, side], dq_send.at[side])


def shards(query, key, value, dout, tile_mask):
    n_ctx, n_uly = lax.axis_size("ctx"), lax.axis_size("uly")
    tok, width = query.shape
    n_heads, _, span = tile_mask.shape
    hd = width // n_heads
    reach = span // 2
    group = reach * BLK // tok
    rows = group * tok
    nb = rows // BLK
    slots = (n_heads + group - 1) // group
    extra = slots * group - n_heads
    full = slots * group * hd

    place = lax.axis_index("ctx") * n_uly + lax.axis_index("uly")
    chunk, member = place // group, place % group
    mask = jnp.pad(tile_mask, ((0, extra), (nb, nb), (0, 0)))
    mask = lax.dynamic_slice(mask, (member * slots, chunk * nb, 0), (slots, 3 * nb, span))
    none = jnp.zeros((slots,), tile_mask.dtype)
    pairs = [
        mask[:, j, nb + i - j + reach] if 0 <= nb + i - j + reach < span else none
        for j in range(3 * nb)
        for i in range(nb)
    ]
    bias = jnp.where(jnp.stack(pairs, 1) != 0, 0.0, NEVER).astype(jnp.float32).reshape(-1)

    arrays = (query, key, value, dout)
    if extra:
        arrays = tuple(jnp.pad(a, ((0, 0), (0, extra * hd))) for a in arrays)
    dims = (n_ctx, n_uly, tok, hd, slots, group)
    stat_rows = (3 * nb + 7) // 8 * 8
    dma = pltpu.SemaphoreType.DMA
    anywhere = pl.BlockSpec(memory_space=pl.ANY)
    outs = pl.pallas_call(
        functools.partial(kernel, dims),
        out_shape=[jax.ShapeDtypeStruct((tok, full), jnp.bfloat16)] * 3,
        in_specs=[pl.BlockSpec(memory_space=pltpu.SMEM)] + [anywhere] * 4,
        out_specs=[anywhere] * 3,
        scratch_shapes=[
            pltpu.VMEM((slots, 2, rows, hd), jnp.bfloat16),
            pltpu.VMEM((slots, 3, 2, rows, hd), jnp.bfloat16),
            pltpu.VMEM((slots, stat_rows, BLK), jnp.float32),
            pltpu.VMEM((slots, 2, stat_rows, BLK), jnp.float32),
            pltpu.VMEM((slots, 2, stat_rows, BLK), jnp.float32),
            pltpu.VMEM((slots, stat_rows, BLK), jnp.float32),
            pltpu.VMEM((slots, 2, stat_rows, BLK), jnp.float32),
            pltpu.VMEM((slots, rows, hd), jnp.float32),
            pltpu.VMEM((slots, 2, rows, hd), jnp.bfloat16),
            pltpu.VMEM((slots, 2, rows, hd), jnp.bfloat16),
            pltpu.VMEM((slots, 3, rows, hd), jnp.bfloat16),
            dma((4,)),
            dma((slots, 4)),
            dma((slots, 4)),
            dma((2,)),
            dma((slots, 2)),
            dma((2,)),
            dma((slots, 2)),
            dma((2,)),
            dma((slots, 2)),
            dma((2,)),
            dma((slots, 2)),
            dma((3,)),
            dma((3,)),
            dma((3,)),
        ],
        compiler_params=pltpu.CompilerParams(
            collective_id=0, has_side_effects=True, vmem_limit_bytes=48 * 2**20
        ),
        cost_estimate=pl.CostEstimate(
            flops=42 * slots * rows * rows * hd,
            bytes_accessed=14 * tok * full,
            transcendentals=6 * slots * rows * rows,
        ),
        name="tile_attention_grad",
    )(bias, *arrays)
    return tuple(o[:, :width] for o in outs)


def solution(mesh):
    rows = P(("ctx", "uly"), None)
    return jax.shard_map(
        shards,
        mesh=mesh,
        in_specs=(rows, rows, rows, rows, P()),
        out_specs=(rows, rows, rows),
        check_vma=False,
    )
```
